32 devices in a mesh: dp: 8 (over z, core), ctx: 4 (over y, x).
Axes of the slice: x: 2, y: 2, z: 4, core: 2. Of those that a mesh axis runs over, the one named last changes fastest.
Arguments:
- activations: bfloat16 [8, 512, 2048], P('dp', 'ctx'), may hold values from -8 to 8
- out_grads: bfloat16 [8, 512, 2048], P('dp', 'ctx'), may hold values from -64 to 64
- segment_ids: int32 [8, 512], P('dp', 'ctx'), may hold values from -1 to 1, as said below
Outputs:
- weight_grad: float32 [2048, 2048], P('ctx', 'dp')
- clip_factors: float32 [8, 2], P('dp')
The draws below stay inside these ranges and needn't reach their ends.
Inputs may be any that keep to these rules, and one draw needn't show every extreme that they name: `segment_ids`: each sequence holds 2 documents, numbered in order; each occupies one or more whole consecutive blocks of 128 tokens, and -1 (padding) occurs only at the end of a document's last block; every document has at least one token.
All inputs are finite; a program needn't handle non-finite values.
Results may differ from the reference program's by a relative error of at most 0.0016.
Values may be sent and summed in bfloat16 or wider, within the bound.
A program may use at most 128 MiB of HBM per device.

```python
import jax
import jax.numpy as jnp
from jax import lax

D_IN = 2048
D_OUT = 2048
BLOCK = 128
SEQ = 512
SEQS = 8
DOCS = 2


pool_factor = 2


def segment_table(key):
    block_count = SEQ // BLOCK

    def one_sequence(seq_key):
        cut_key, pad_key = jax.random.split(seq_key)
        shuffled = jax.random.permutation(cut_key, block_count - 1) + 1
        cuts = jnp.sort(shuffled[:DOCS - 1])
        block_index = jnp.arange(block_count)
        block_doc = jnp.sum(block_index[:, None] >= cuts[None, :], axis=1).astype(jnp.int32)
        next_doc = jnp.concatenate([block_doc[1:], jnp.full((1,), DOCS, jnp.int32)])
        last_block = next_doc != block_doc
        padding = jax.random.randint(pad_key, (block_count,), 0, BLOCK)
        token_block = jnp.arange(SEQ) // BLOCK
        in_block = jnp.arange(SEQ) % BLOCK
        is_padding = last_block[token_block] & (in_block >= BLOCK - padding[token_block])
        return jnp.where(is_padding, -1, block_doc[token_block]).astype(jnp.int32)
    seq_keys = jax.random.split(key, SEQS)
    return jax.vmap(one_sequence)(seq_keys)


def draw_segment_ids(key, part):
    return segment_table(jax.random.fold_in(key, 17))


def atom_table(key):
    pool = pool_factor * BLOCK
    seq_ids = segment_table(jax.random.fold_in(key, 17))
    picks = jax.random.randint(jax.random.fold_in(key, 53), (SEQS, SEQ), 0, pool).astype(jnp.int32)
    return (jnp.maximum(seq_ids, 0) * pool + picks).astype(jnp.int32)


def document_mixture(key, width, basis_tag, noise_tag):
    pool = pool_factor * BLOCK
    atoms = atom_table(key)
    basis_keys = jax.random.split(jax.random.fold_in(key, basis_tag), SEQS)
    noise_keys = jax.random.split(jax.random.fold_in(key, noise_tag), SEQS)
    share = 0.5

    def one_sequence(inputs):
        atom_row, basis_key, noise_key = inputs
        basis = jax.random.normal(basis_key, (DOCS * pool, width), jnp.float32)
        noise = jax.random.truncated_normal(noise_key, -4.0, 4.0, (SEQ, width), jnp.float32)
        shared = jnp.take(basis, atom_row, axis=0)
        return jnp.sqrt(1.0 - share) * noise + jnp.sqrt(share) * shared
    mixed = lax.map(one_sequence, (atoms, basis_keys, noise_keys))
    return (mixed, share)


def draw_activations(key, part):
    mixed, share = document_mixture(key, D_IN, 31, 37)
    return jnp.clip(mixed, -8.0, 8.0).astype(jnp.bfloat16)


def draw_out_grads(key, part):
    mixed, share = document_mixture(key, D_OUT, 41, 43)
    typical = 2.0 * BLOCK
    pool = pool_factor * BLOCK
    spread = 1.0 + typical * share * share / pool
    scale = 600.0 / jnp.sqrt(jnp.float32(D_IN) * jnp.float32(D_OUT) * typical * spread)
    values = mixed * scale
    return jnp.clip(values, -64.0, 64.0).astype(jnp.bfloat16)


def setup_inputs(seed: int = 0) -> dict:
    keys = jax.random.split(jax.random.key(seed), 4)
    activations = draw_activations(jax.random.fold_in(keys[3], 71), 0)
    out_grads = draw_out_grads(jax.random.fold_in(keys[3], 71), 0)
    segment_ids = draw_segment_ids(jax.random.fold_in(keys[3], 71), 0)
    return dict(activations=activations, out_grads=out_grads, segment_ids=segment_ids)


clip_bound = 600.0

def reference(activations, out_grads, segment_ids):
    doc_range = jnp.arange(DOCS, dtype=jnp.int32)

    def one_sequence(grad_total, inputs):
        seq_acts, seq_grads, seq_ids = inputs
        gram_in = jnp.dot(seq_acts, seq_acts.T, preferred_element_type=jnp.float32)
        gram_out = jnp.dot(seq_grads, seq_grads.T, preferred_element_type=jnp.float32)
        same_doc = (seq_ids[:, None] == seq_ids[None, :]) & (seq_ids[:, None] >= 0)
        per_token = lax.optimization_barrier(jnp.sum(jnp.where(same_doc, gram_in * gram_out, jnp.float32(0.0)), axis=1))
        one_hot = (seq_ids[:, None] == doc_range[None, :]).astype(jnp.float32)
        norm_sq = jnp.dot(per_token, one_hot, precision=lax.Precision.HIGHEST)
        clip_factor = clip_bound / jnp.sqrt(jnp.maximum(norm_sq, clip_bound * clip_bound))
        token_clip = jnp.dot(one_hot, clip_factor, precision=lax.Precision.HIGHEST)
        scaled = (seq_grads.astype(jnp.float32) * token_clip[:, None]).astype(jnp.bfloat16)
        partial_grad = lax.dot_general(seq_acts, scaled, (((0,), (0,)), ((), ())), preferred_element_type=jnp.float32)
        return (grad_total + partial_grad, clip_factor)
    start_grad = jnp.zeros((D_IN, D_OUT), jnp.float32)
    weight_grad, clip_factors = lax.scan(one_sequence, start_grad, (activations, out_grads, segment_ids))
    return (weight_grad, clip_factors)
```

```python
import functools

import jax
import jax.numpy as jnp
from jax import lax
from jax.experimental import pallas as pl
from jax.experimental.pallas import tpu as pltpu
from jax.sharding import PartitionSpec as P

BLOCK = 128
LANES = 128
GROUP = 4

clip_bound = 600.0


def plain_body(activations, out_grads, segment_ids):
    own_acts = activations[0]
    own_grads = out_grads[0]
    own_ids = segment_ids[0]
    groups = lax.axis_size("ctx")
    my_slot = lax.axis_index("ctx")
    row_count = own_acts.shape[1] // groups
    all_ids = lax.all_gather(own_ids, "ctx", axis=0, tiled=True)
    doc_count = all_ids.shape[0] // BLOCK // 2
    doc_range = jnp.arange(doc_count, dtype=jnp.int32)
    own_hot = (own_ids[:, None] == doc_range[None, :]).astype(jnp.float32)
    all_acts = lax.all_gather(own_acts, "ctx", axis=0, tiled=True)
    all_grads = lax.all_gather(own_grads, "ctx", axis=0, tiled=True)
    gram_in = lax.dot_general(
        own_acts, all_acts, (((1,), (1,)), ((), ())), preferred_element_type=jnp.float32
    )
    gram_out = lax.dot_general(
        own_grads, all_grads, (((1,), (1,)), ((), ())), preferred_element_type=jnp.float32
    )
    same_doc = (own_ids[:, None] == all_ids[None, :]) & (own_ids[:, None] >= 0)
    per_token = jnp.sum(jnp.where(same_doc, gram_in * gram_out, jnp.float32(0.0)), axis=1)
    norm_sq = lax.psum(jnp.dot(per_token, own_hot, precision=lax.Precision.HIGHEST), "ctx")
    clip_factor = clip_bound / jnp.sqrt(jnp.maximum(norm_sq, clip_bound * clip_bound))
    own_rows = lax.dynamic_slice_in_dim(all_acts, my_slot * row_count, row_count, 1)
    all_hot = (all_ids[:, None] == doc_range[None, :]).astype(jnp.float32)
    token_clip = jnp.dot(all_hot, clip_factor, precision=lax.Precision.HIGHEST)
    scaled = (all_grads.astype(jnp.float32) * token_clip[:, None]).astype(jnp.bfloat16)
    partial_grad = lax.dot_general(
        own_rows, scaled, (((0,), (0,)), ((), ())), preferred_element_type=jnp.float32
    )
    weight_grad = lax.psum_scatter(partial_grad, "dp", scatter_dimension=1, tiled=True)
    return (weight_grad, clip_factor[None, :])


def kernel(docs, his, n, a_ref, g_ref, id_ref, out_ref, clip_ref,
           acts, grads, staged, ids, shares, scaled, outgoing, incoming,
           sa_plane, sa_z, sa_sib, sa_fwd, ra, sg_split, sg_a, sg_b, sg_fwd, rg,
           s_id, r_id, s_norm, r_norm, s_out, r_out):
    R = GROUP
    dp = lax.axis_index("dp")
    c = lax.axis_index("ctx")
    hi = dp // R
    r = lax.rem(dp, R)
    base = hi * R
    rows = acts.shape[3]
    width = out_ref.shape[1]

    def flip(v, bits):
        out = v
        for bit in (1, 2):
            if bits & bit:
                has = lax.rem(out // bit, 2)
                out = out + bit * (1 - 2 * has)
        return out

    rx = [flip(r, b) for b in range(R)]
    cx = [flip(c, b) for b in range(n)]
    peers = [(rb, cb) for rb in range(R) for cb in range(n) if rb or cb]

    barrier = pltpu.get_barrier_semaphore()
    for rb, cb in peers:
        pl.semaphore_signal(barrier, inc=1, device_id=(base + rx[rb], cx[cb]),
                            device_id_type=pl.DeviceIdType.MESH)
    others = []
    for h in range(1, his):
        there = lax.rem(hi + h, his)
        others.append(there * R + r)
        pl.semaphore_signal(barrier, inc=1, device_id=(others[-1], c),
                            device_id_type=pl.DeviceIdType.MESH)

    tok = id_ref[...]
    keep = jnp.transpose(jnp.broadcast_to((tok >= 0).astype(jnp.float32), (BLOCK, BLOCK)))
    keep = jnp.concatenate([keep] * (width // LANES), axis=1) > 0.5
    for q in range(R):
        for p in range(his):
            block = lax.rem(hi + 1 + p, his) * R + q
            piece = g_ref[:, pl.ds(pl.multiple_of(block * width, LANES), width)]
            staged[q, :, p * width:(p + 1) * width] = jnp.where(
                keep, piece.astype(jnp.float32), 0.0).astype(jnp.bfloat16)
    ids[r, c] = tok
    grads[r, c] = staged[r]
    acts[r, c] = a_ref[:, pl.ds(pl.multiple_of(c * rows, LANES), rows)]

    pl.semaphore_wait(barrier, len(peers) + his - 1)

    started = []

    def send(src, dst, ssem, rsem, to):
        cp = pltpu.make_async_remote_copy(src_ref=src, dst_ref=dst, send_sem=ssem, recv_sem=rsem,
                                          device_id=to, device_id_type=pl.DeviceIdType.MESH)
        cp.start()
        started.append(cp)

    def arrive(dst, rsem):
        pltpu.make_async_copy(dst, dst, rsem).wait()

    for b in (2, 3, 1):
        send(staged.at[rx[b]], grads.at[r, c], sg_split.at[b], rg.at[r, c], (base + rx[b], c))
    for b in (1, 2, 3):
        cols = pl.ds(pl.multiple_of(cx[b] * rows, LANES), rows)
        send(a_ref.at[:, cols], acts.at[r, c], sa_plane.at[b], ra.at[r, c], (dp, cx[b]))
    for k, (rb, cb) in enumerate(peers):
        send(ids.at[r, c], ids.at[r, c], s_id.at[k], r_id.at[rb, cb], (base + rx[rb], cx[cb]))

    def pass_acts(cb):
        slot = acts.at[r, cx[cb]]
        send(slot, slot, sa_z.at[cb], ra.at[r, cx[cb]], (base + rx[2], c))
        send(slot, slot, sa_sib.at[cb], ra.at[r, cx[cb]], (base + rx[1], c))

    def gather_grads(rb):
        slot = grads.at[rx[rb], c]
        send(slot, slot, sg_a.at[rb], rg.at[rx[rb], c], (dp, cx[1]))
        send(slot, slot, sg_b.at[rb], rg.at[rx[rb], c], (dp, cx[2]))

    def forward_grads(rb):
        came, to = (1, 2) if rb in (0, 2) else (2, 1)
        slot = grads.at[rx[rb], cx[came]]
        arrive(slot, rg.at[rx[rb], cx[came]])
        send(slot, slot, sg_fwd.at[rb], rg.at[rx[rb], cx[came]], (dp, cx[to]))

    def forward_acts(cb):
        slot = acts.at[rx[2], cx[cb]]
        arrive(slot, ra.at[rx[2], cx[cb]])
        send(slot, slot, sa_fwd.at[cb], ra.at[rx[2], cx[cb]], (base + rx[1], c))

    gather_grads(0)
    pass_acts(0)
    for b in (1, 2, 3):
        arrive(grads.at[rx[b], c], rg.at[rx[b], c])
        gather_grads(b)
        arrive(acts.at[r, cx[b]], ra.at[r, cx[b]])
        pass_acts(b)
    for b in (0, 1, 2, 3):
        forward_acts(b)
        forward_grads(b)

    for rb, cb in peers:
        arrive(ids.at[rx[rb], cx[cb]], r_id.at[rb, cb])
    for cb in range(n):
        for rb in (1, 3):
            arrive(acts.at[rx[rb], cx[cb]], ra.at[rx[rb], cx[cb]])
    for rb in range(R):
        for cb in ((2, 3) if rb in (0, 2) else (1, 3)):
            arrive(grads.at[rx[rb], cx[cb]], rg.at[rx[rb], cx[cb]])

    seq = n * BLOCK
    wide = acts.shape[3]
    cols = grads.shape[3]
    table = shares.shape[2:]
    row_at = lax.broadcasted_iota(jnp.int32, table, 0)
    nt = (((1,), (1,)), ((), ()))

    def doc_rows(s):
        return [jnp.broadcast_to(jnp.max(ids[s, i], axis=1, keepdims=True), (1, BLOCK))
                for i in range(n)]

    def norm_step(s, total):
        A = acts[s].reshape(seq, wide)
        G = grads[s].reshape(seq, cols)
        prod = (lax.dot_general(A, A, nt, preferred_element_type=jnp.float32)
                * lax.dot_general(G, G, nt, preferred_element_type=jnp.float32))
        dr = doc_rows(s)
        along = jnp.concatenate(dr, axis=1)
        v = jnp.zeros((1, seq), jnp.float32)
        for i in range(n):
            u = jnp.sum(prod[i * BLOCK:(i + 1) * BLOCK], axis=0, keepdims=True)
            mine = jnp.concatenate([dr[i]] * n, axis=1)
            v = v + jnp.where(along == mine, u, 0.0)
        for b in range(docs):
            nb = jnp.sum(jnp.where(along == b, v, 0.0), axis=1, keepdims=True)
            total = jnp.where(row_at == s * docs + b, jnp.broadcast_to(nb, table), total)
        return total

    total = lax.fori_loop(0, R, norm_step, jnp.zeros(table, jnp.float32))
    shares[r, c] = total
    for k, (rb, cb) in enumerate(peers):
        send(shares.at[r, c], shares.at[r, c], s_norm.at[k], r_norm.at[rb, cb],
             (base + rx[rb], cx[cb]))
    for rb, cb in peers:
        arrive(shares.at[rx[rb], cx[cb]], r_norm.at[rb, cb])
    norm = jnp.zeros(table, jnp.float32)
    for i in range(R):
        for j in range(n):
            norm = norm + shares[i, j]
    clip = clip_bound / jnp.sqrt(jnp.maximum(norm, clip_bound * clip_bound))

    lane_at = lax.broadcasted_iota(jnp.int32, (1, LANES), 1)
    own = jnp.zeros((1, LANES), jnp.float32)
    for b in range(docs):
        picked = jnp.sum(jnp.where(row_at == r * docs + b, clip, 0.0), axis=0, keepdims=True)
        own = jnp.where(lane_at == b, picked, own)
    clip_ref[...] = own[:, :docs]

    for s in range(R):
        dr = doc_rows(s)
        for i in range(n):
            factor = jnp.zeros((1, LANES), jnp.float32)
            for b in range(docs):
                factor = jnp.where(dr[i] == b, clip[s * docs + b:s * docs + b + 1], factor)
            factor = jnp.concatenate([factor] * (cols // LANES), axis=1)
            at = (s * n + i) * BLOCK
            scaled[at:at + BLOCK] = (grads[s, i].astype(jnp.float32) * factor).astype(jnp.bfloat16)

    tn = (((0,), (0,)), ((), ()))
    whole = acts[...].reshape(R * seq, wide)
    for p in range(his):
        part = lax.dot_general(whole, scaled[:, p * width:(p + 1) * width], tn,
                               preferred_element_type=jnp.float32)
        if p < his - 1:
            outgoing[p] = part.astype(jnp.bfloat16)
            send(outgoing.at[p], incoming.at[p], s_out.at[p], r_out.at[p], (others[p], c))
        else:
            out_ref[...] = part
    for p in range(his - 1):
        arrive(incoming.at[p], r_out.at[p])
        out_ref[...] += incoming[p].astype(jnp.float32)
    for cp in started:
        cp.wait_send()


def group_body(activations, out_grads, segment_ids):
    n = lax.axis_size("ctx")
    size = lax.axis_size("dp")
    his = size // GROUP
    tokens, d_in = activations.shape[1:]
    d_out = out_grads.shape[2]
    rows, width = d_in // n, d_out // size
    docs = n * tokens // BLOCK // 2
    table = -(-GROUP * docs // 8) * 8
    bf, f32 = jnp.bfloat16, jnp.float32
    dma = pltpu.SemaphoreType.DMA
    vm = pl.BlockSpec(memory_space=pltpu.VMEM)
    peers = GROUP * n - 1
    return pl.pallas_call(
        functools.partial(kernel, docs, his, n),
        out_shape=(jax.ShapeDtypeStruct((rows, width), f32), jax.ShapeDtypeStruct((1, docs), f32)),
        in_specs=[vm, vm, vm],
        out_specs=(vm, vm),
        scratch_shapes=[
            pltpu.VMEM((GROUP, n, tokens, rows), bf),
            pltpu.VMEM((GROUP, n, tokens, his * width), bf),
            pltpu.VMEM((GROUP, tokens, his * width), bf),
            pltpu.VMEM((GROUP, n, 1, tokens), jnp.int32),
            pltpu.VMEM((GROUP, n, table, LANES), f32),
            pltpu.VMEM((GROUP * n * tokens, his * width), bf),
            pltpu.VMEM((his - 1, rows, width), bf),
            pltpu.VMEM((his - 1, rows, width), bf),
            dma((n,)), dma((n,)), dma((n,)), dma((n,)), dma((GROUP, n)),
            dma((GROUP,)), dma((GROUP,)), dma((GROUP,)), dma((GROUP,)), dma((GROUP, n)),
            dma((peers,)), dma((GROUP, n)), dma((peers,)), dma((GROUP, n)),
            dma((his - 1,)), dma((his - 1,)),
        ],
        compiler_params=pltpu.CompilerParams(
            collective_id=0, has_side_effects=True, vmem_limit_bytes=48 * 1024 * 1024),
    )(activations[0], out_grads[0], segment_ids)


def body(activations, out_grads, segment_ids):
    n = lax.axis_size("ctx")
    size = lax.axis_size("dp")
    rows, width = activations.shape[2] // n, out_grads.shape[2] // size
    fits = (n == GROUP and size % GROUP == 0 and size > GROUP and activations.shape[1] == BLOCK
            and rows % LANES == 0 and width % LANES == 0)
    chosen = group_body if fits else plain_body
    return chosen(activations, out_grads, segment_ids)


def solution(mesh):
    placed = (P("dp", "ctx", None), P("dp", "ctx", None), P("dp", "ctx"))
    return jax.shard_map(
        body, mesh=mesh, in_specs=placed, out_specs=(P("ctx", "dp"), P("dp", None)), check_vma=False
    )
```

```python
import functools

import jax
import jax.numpy as jnp
from jax import lax
from jax.experimental import pallas as pl
from jax.experimental.pallas import tpu as pltpu
from jax.sharding import PartitionSpec as P

BLOCK = 128
LANES = 128
GROUP = 4

clip_bound = 600.0


def plain_body(activations, out_grads, segment_ids):
    own_acts = activations[0]
    own_grads = out_grads[0]
    own_ids = segment_ids[0]
    groups = lax.axis_size("ctx")
    my_slot = lax.axis_index("ctx")
    row_count = own_acts.shape[1] // groups
    all_ids = lax.all_gather(own_ids, "ctx", axis=0, tiled=True)
    doc_count = all_ids.shape[0] // BLOCK // 2
    doc_range = jnp.arange(doc_count, dtype=jnp.int32)
    own_hot = (own_ids[:, None] == doc_range[None, :]).astype(jnp.float32)
    all_acts = lax.all_gather(own_acts, "ctx", axis=0, tiled=True)
    all_grads = lax.all_gather(own_grads, "ctx", axis=0, tiled=True)
    gram_in = lax.dot_general(
        own_acts, all_acts, (((1,), (1,)), ((), ())), preferred_element_type=jnp.float32
    )
    gram_out = lax.dot_general(
        own_grads, all_grads, (((1,), (1,)), ((), ())), preferred_element_type=jnp.float32
    )
    same_doc = (own_ids[:, None] == all_ids[None, :]) & (own_ids[:, None] >= 0)
    per_token = jnp.sum(jnp.where(same_doc, gram_in * gram_out, jnp.float32(0.0)), axis=1)
    norm_sq = lax.psum(jnp.dot(per_token, own_hot, precision=lax.Precision.HIGHEST), "ctx")
    clip_factor = clip_bound / jnp.sqrt(jnp.maximum(norm_sq, clip_bound * clip_bound))
    own_rows = lax.dynamic_slice_in_dim(all_acts, my_slot * row_count, row_count, 1)
    all_hot = (all_ids[:, None] == doc_range[None, :]).astype(jnp.float32)
    token_clip = jnp.dot(all_hot, clip_factor, precision=lax.Precision.HIGHEST)
    scaled = (all_grads.astype(jnp.float32) * token_clip[:, None]).astype(jnp.bfloat16)
    partial_grad = lax.dot_general(
        own_rows, scaled, (((0,), (0,)), ((), ())), preferred_element_type=jnp.float32
    )
    weight_grad = lax.psum_scatter(partial_grad, "dp", scatter_dimension=1, tiled=True)
    return (weight_grad, clip_factor[None, :])


def kernel(docs, his, n, a_ref, g_ref, id_ref, out_ref, clip_ref,
           acts, grads, raw, staged, ids, shares, turned, gram_in, scaled, outgoing, incoming, s_own,
           sa_plane, sa_z, sa_sib, sa_fwd, ra, sg_split, sg_a, sg_b, sg_fwd, rg,
           s_id, r_id, s_norm, r_norm, s_out, r_out):
    R = GROUP
    dp = lax.axis_index("dp")
    c = lax.axis_index("ctx")
    hi = dp // R
    r = lax.rem(dp, R)
    base = hi * R
    rows = acts.shape[3]
    width = out_ref.shape[1]

    def flip(v, bits):
        out = v
        for bit in (1, 2):
            if bits & bit:
                has = lax.rem(out // bit, 2)
                out = out + bit * (1 - 2 * has)
        return out

    rx = [flip(r, b) for b in range(R)]
    cx = [flip(c, b) for b in range(n)]
    peers = [(rb, cb) for rb in range(R) for cb in range(n) if rb or cb]

    local = [
        pltpu.make_async_copy(id_ref, ids.at[r, c], s_own.at[0]),
        pltpu.make_async_copy(g_ref.at[0], raw, s_own.at[1]),
        pltpu.make_async_copy(
            a_ref.at[0, :, pl.ds(pl.multiple_of(c * rows, LANES), rows)], acts.at[r, c], s_own.at[2]),
    ]
    for cp in local:
        cp.start()
    barrier = pltpu.get_barrier_semaphore()
    for rb, cb in peers:
        pl.semaphore_signal(barrier, inc=1, device_id=(base + rx[rb], cx[cb]),
                            device_id_type=pl.DeviceIdType.MESH)
    others = []
    for h in range(1, his):
        there = lax.rem(hi + h, his)
        others.append(there * R + rx[2])
        pl.semaphore_signal(barrier, inc=1, device_id=(others[-1], c),
                            device_id_type=pl.DeviceIdType.MESH)

    local[0].wait()
    tok = ids[r, c]
    keep = jnp.transpose(jnp.broadcast_to((tok >= 0).astype(jnp.float32), (BLOCK, BLOCK)))
    keep = jnp.concatenate([keep] * (width // LANES), axis=1) > 0.5
    local[1].wait()
    for q in range(R):
        for p in range(his):
            there = lax.rem(hi + 1 + p, his)
            block = there * R + (q if p == his - 1 else q ^ 2)
            piece = raw[:, pl.ds(pl.multiple_of(block * width, LANES), width)]
            staged[q, :, p * width:(p + 1) * width] = jnp.where(
                keep, piece.astype(jnp.float32), 0.0).astype(jnp.bfloat16)
    grads[r, c] = staged[r]
    local[2].wait()

    pl.semaphore_wait(barrier, len(peers) + his - 1)

    started = []

    def send(src, dst, ssem, rsem, to):
        cp = pltpu.make_async_remote_copy(src_ref=src, dst_ref=dst, send_sem=ssem, recv_sem=rsem,
                                          device_id=to, device_id_type=pl.DeviceIdType.MESH)
        cp.start()
        started.append(cp)

    def arrive(dst, rsem):
        pltpu.make_async_copy(dst, dst, rsem).wait()

    for b in (2, 3, 1):
        send(staged.at[rx[b]], grads.at[r, c], sg_split.at[b], rg.at[r, c], (base + rx[b], c))
    for b in (1, 2, 3):
        cols = pl.ds(pl.multiple_of(cx[b] * rows, LANES), rows)
        send(a_ref.at[0, :, cols], acts.at[r, c], sa_plane.at[b], ra.at[r, c], (dp, cx[b]))
    for k, (rb, cb) in enumerate(peers):
        send(ids.at[r, c], ids.at[r, c], s_id.at[k], r_id.at[rb, cb], (base + rx[rb], cx[cb]))

    def pass_acts(cb):
        slot = acts.at[r, cx[cb]]
        send(slot, slot, sa_z.at[cb], ra.at[r, cx[cb]], (base + rx[2], c))
        send(slot, slot, sa_sib.at[cb], ra.at[r, cx[cb]], (base + rx[1], c))

    def gather_grads(rb):
        slot = grads.at[rx[rb], c]
        send(slot, slot, sg_a.at[rb], rg.at[rx[rb], c], (dp, cx[1]))
        send(slot, slot, sg_b.at[rb], rg.at[rx[rb], c], (dp, cx[2]))

    def forward_grads(rb):
        came, to = (1, 2) if rb in (0, 2) else (2, 1)
        slot = grads.at[rx[rb], cx[came]]
        arrive(slot, rg.at[rx[rb], cx[came]])
        send(slot, slot, sg_fwd.at[rb], rg.at[rx[rb], cx[came]], (dp, cx[to]))

    def forward_acts(cb):
        slot = acts.at[rx[2], cx[cb]]
        arrive(slot, ra.at[rx[2], cx[cb]])
        send(slot, slot, sa_fwd.at[cb], ra.at[rx[2], cx[cb]], (base + rx[1], c))

    gather_grads(0)
    pass_acts(0)
    for b in (1, 2, 3):
        arrive(grads.at[rx[b], c], rg.at[rx[b], c])
        gather_grads(b)
        arrive(acts.at[r, cx[b]], ra.at[r, cx[b]])
        pass_acts(b)
    seq = n * BLOCK
    wide = acts.shape[3]
    cols = grads.shape[3]
    pieces, step = outgoing.shape[1:3]
    table = shares.shape[2:]
    row_at = lax.broadcasted_iota(jnp.int32, table, 0)
    nt = (((1,), (1,)), ((), ()))

    def doc_rows(s):
        return [jnp.broadcast_to(jnp.max(ids[s, i], axis=1, keepdims=True), (1, BLOCK))
                for i in range(n)]

    def prepare(rb):
        s = rx[rb]
        for i in range(n):
            at = pl.multiple_of((s * n + i) * BLOCK, LANES)
            turned[:, pl.ds(at, BLOCK)] = jnp.transpose(acts[s, i])
        A = acts[s].reshape(seq, wide)
        gram = lax.dot_general(A, A, nt, preferred_element_type=jnp.float32)
        dr = doc_rows(s)
        along = jnp.concatenate(dr, axis=1)
        for i in range(n):
            mine = jnp.concatenate([dr[i]] * n, axis=1)
            at = slice(i * BLOCK, (i + 1) * BLOCK)
            gram_in[rb, at] = jnp.where(along == mine, gram[at], 0.0)

    def norm_step(rb, total):
        s = rx[rb]
        for cb in ((2, 3) if rb in (0, 2) else (1, 3)):
            arrive(grads.at[s, cx[cb]], rg.at[s, cx[cb]])
        G = grads[s].reshape(seq, cols)
        gram_out = lax.dot_general(G, G, nt, preferred_element_type=jnp.float32)
        v = jnp.sum(gram_in[rb] * gram_out, axis=0, keepdims=True)
        along = jnp.concatenate(doc_rows(s), axis=1)
        for b in range(docs):
            nb = jnp.sum(jnp.where(along == b, v, 0.0), axis=1, keepdims=True)
            total = jnp.where(row_at == s * docs + b, jnp.broadcast_to(nb, table), total)
        return total

    for b in range(n):
        forward_acts(b)
    for rb, cb in peers:
        arrive(ids.at[rx[rb], cx[cb]], r_id.at[rb, cb])
    for rb in (0, 2, 1, 3):
        if rb in (1, 3):
            for cb in range(n):
                arrive(acts.at[rx[rb], cx[cb]], ra.at[rx[rb], cx[cb]])
        forward_grads({0: 0, 2: 1, 1: 2, 3: 3}[rb])
        prepare(rb)
    total = jnp.zeros(table, jnp.float32)
    for rb in range(R):
        total = norm_step(rb, total)
    shares[r, c] = total
    for k, (rb, cb) in enumerate(peers):
        send(shares.at[r, c], shares.at[r, c], s_norm.at[k], r_norm.at[rb, cb],
             (base + rx[rb], cx[cb]))
    for rb, cb in peers:
        arrive(shares.at[rx[rb], cx[cb]], r_norm.at[rb, cb])
    norm = jnp.zeros(table, jnp.float32)
    for i in range(R):
        for j in range(n):
            norm = norm + shares[i, j]
    clip = clip_bound / jnp.sqrt(jnp.maximum(norm, clip_bound * clip_bound))

    lane_at = lax.broadcasted_iota(jnp.int32, (1, LANES), 1)
    own = jnp.zeros((1, LANES), jnp.float32)
    for b in range(docs):
        picked = jnp.sum(jnp.where(row_at == r * docs + b, clip, 0.0), axis=0, keepdims=True)
        own = jnp.where(lane_at == b, picked, own)
    clip_ref[...] = own[:, :docs]

    factors = []
    for s in range(R):
        dr = doc_rows(s)
        for i in range(n):
            factor = jnp.zeros((1, LANES), jnp.float32)
            for b in range(docs):
                factor = jnp.where(dr[i] == b, clip[s * docs + b:s * docs + b + 1], factor)
            factors.append(jnp.concatenate([factor] * (width // LANES), axis=1))

    def scale(p):
        at_cols = slice(p * width, (p + 1) * width)
        for k, factor in enumerate(factors):
            piece = grads[k // n, k % n, :, at_cols].astype(jnp.float32) * factor
            scaled[k * BLOCK:(k + 1) * BLOCK, at_cols] = piece.astype(jnp.bfloat16)

    for p in range(his - 1):
        scale(p)
        for k in range(pieces):
            at = slice(k * step, (k + 1) * step)
            outgoing[p, k] = jnp.dot(turned[at], scaled[:, p * width:(p + 1) * width],
                                     preferred_element_type=jnp.float32).astype(jnp.bfloat16)
            send(outgoing.at[p, k], incoming.at[p, k], s_out.at[p, k], r_out.at[p, k],
                 (others[p], c))
    scale(his - 1)
    out_ref[...] = jnp.dot(turned[...], scaled[:, (his - 1) * width:],
                           preferred_element_type=jnp.float32)
    for p in range(his - 1):
        for k in range(pieces):
            arrive(incoming.at[p, k], r_out.at[p, k])
            out_ref[k * step:(k + 1) * step] += incoming[p, k].astype(jnp.float32)
    for cp in started:
        cp.wait_send()


def group_body(activations, out_grads, segment_ids):
    n = lax.axis_size("ctx")
    size = lax.axis_size("dp")
    his = size // GROUP
    tokens, d_in = activations.shape[1:]
    d_out = out_grads.shape[2]
    rows, width = d_in // n, d_out // size
    docs = n * tokens // BLOCK // 2
    table = -(-GROUP * docs // 8) * 8
    bf, f32 = jnp.bfloat16, jnp.float32
    dma = pltpu.SemaphoreType.DMA
    vm = pl.BlockSpec(memory_space=pltpu.VMEM)
    hbm = pl.BlockSpec(memory_space=pltpu.HBM)
    pieces = rows // LANES
    peers = GROUP * n - 1
    return pl.pallas_call(
        functools.partial(kernel, docs, his, n),
        out_shape=(jax.ShapeDtypeStruct((rows, width), f32), jax.ShapeDtypeStruct((1, docs), f32)),
        in_specs=[hbm, hbm, hbm],
        out_specs=(vm, vm),
        scratch_shapes=[
            pltpu.VMEM((GROUP, n, tokens, rows), bf),
            pltpu.VMEM((GROUP, n, tokens, his * width), bf),
            pltpu.VMEM((tokens, his * GROUP * width), bf),
            pltpu.VMEM((GROUP, tokens, his * width), bf),
            pltpu.VMEM((GROUP, n, 1, tokens), jnp.int32),
            pltpu.VMEM((GROUP, n, table, LANES), f32),
            pltpu.VMEM((rows, GROUP * n * tokens), bf),
            pltpu.VMEM((GROUP, n * tokens, n * tokens), f32),
            pltpu.VMEM((GROUP * n * tokens, his * width), bf),
            pltpu.VMEM((his - 1, pieces, rows // pieces, width), bf),
            pltpu.VMEM((his - 1, pieces, rows // pieces, width), bf),
            dma((3,)),
            dma((n,)), dma((n,)), dma((n,)), dma((n,)), dma((GROUP, n)),
            dma((GROUP,)), dma((GROUP,)), dma((GROUP,)), dma((GROUP,)), dma((GROUP, n)),
            dma((peers,)), dma((GROUP, n)), dma((peers,)), dma((GROUP, n)),
            dma((his - 1, pieces)), dma((his - 1, pieces)),
        ],
        compiler_params=pltpu.CompilerParams(
            collective_id=0, has_side_effects=True, vmem_limit_bytes=53 * 1024 * 1024),
    )(activations, out_grads, segment_ids)


def body(activations, out_grads, segment_ids):
    n = lax.axis_size("ctx")
    size = lax.axis_size("dp")
    rows, width = activations.shape[2] // n, out_grads.shape[2] // size
    fits = (n == GROUP and size % GROUP == 0 and size > GROUP and activations.shape[1] == BLOCK
            and rows % LANES == 0 and width % LANES == 0)
    chosen = group_body if fits else plain_body
    return chosen(activations, out_grads, segment_ids)


def solution(mesh):
    placed = (P("dp", "ctx", None), P("dp", "ctx", None), P("dp", "ctx"))
    return jax.shard_map(
        body, mesh=mesh, in_specs=placed, out_specs=(P("ctx", "dp"), P("dp", None)), check_vma=False
    )
```

```python
import functools

import jax
import jax.numpy as jnp
from jax import lax
from jax.experimental import pallas as pl
from jax.experimental.pallas import tpu as pltpu
from jax.sharding import PartitionSpec as P

BLOCK = 128
LANES = 128
GROUP = 4

clip_bound = 600.0


def plain_body(activations, out_grads, segment_ids):
    own_acts = activations[0]
    own_grads = out_grads[0]
    own_ids = segment_ids[0]
    groups = lax.axis_size("ctx")
    my_slot = lax.axis_index("ctx")
    row_count = own_acts.shape[1] // groups
    all_ids = lax.all_gather(own_ids, "ctx", axis=0, tiled=True)
    doc_count = all_ids.shape[0] // BLOCK // 2
    doc_range = jnp.arange(doc_count, dtype=jnp.int32)
    own_hot = (own_ids[:, None] == doc_range[None, :]).astype(jnp.float32)
    all_acts = lax.all_gather(own_acts, "ctx", axis=0, tiled=True)
    all_grads = lax.all_gather(own_grads, "ctx", axis=0, tiled=True)
    gram_in = lax.dot_general(
        own_acts, all_acts, (((1,), (1,)), ((), ())), preferred_element_type=jnp.float32
    )
    gram_out = lax.dot_general(
        own_grads, all_grads, (((1,), (1,)), ((), ())), preferred_element_type=jnp.float32
    )
    same_doc = (own_ids[:, None] == all_ids[None, :]) & (own_ids[:, None] >= 0)
    per_token = jnp.sum(jnp.where(same_doc, gram_in * gram_out, jnp.float32(0.0)), axis=1)
    norm_sq = lax.psum(jnp.dot(per_token, own_hot, precision=lax.Precision.HIGHEST), "ctx")
    clip_factor = clip_bound / jnp.sqrt(jnp.maximum(norm_sq, clip_bound * clip_bound))
    own_rows = lax.dynamic_slice_in_dim(all_acts, my_slot * row_count, row_count, 1)
    all_hot = (all_ids[:, None] == doc_range[None, :]).astype(jnp.float32)
    token_clip = jnp.dot(all_hot, clip_factor, precision=lax.Precision.HIGHEST)
    scaled = (all_grads.astype(jnp.float32) * token_clip[:, None]).astype(jnp.bfloat16)
    partial_grad = lax.dot_general(
        own_rows, scaled, (((0,), (0,)), ((), ())), preferred_element_type=jnp.float32
    )
    weight_grad = lax.psum_scatter(partial_grad, "dp", scatter_dimension=1, tiled=True)
    return (weight_grad, clip_factor[None, :])


def kernel(docs, his, n, a_ref, g_ref, id_ref, out_ref, clip_ref,
           acts, grads, raw, staged, ids, shares, turned, gram_in, scaled, outgoing, incoming, s_own,
           sa_plane, sa_z, sa_sib, sa_fwd, ra, sg_split, sg_a, sg_b, sg_fwd, rg,
           s_id, r_id, s_norm, r_norm, s_out, r_out):
    R = GROUP
    dp = lax.axis_index("dp")
    c = lax.axis_index("ctx")
    hi = dp // R
    r = lax.rem(dp, R)
    base = hi * R
    rows = acts.shape[3]
    width = out_ref.shape[1]

    def flip(v, bits):
        out = v
        for bit in (1, 2):
            if bits & bit:
                has = lax.rem(out // bit, 2)
                out = out + bit * (1 - 2 * has)
        return out

    rx = [flip(r, b) for b in range(R)]
    cx = [flip(c, b) for b in range(n)]
    peers = [(rb, cb) for rb in (2, 3, 0, 1) for cb in (3, 2, 1, 0) if rb or cb]

    local = [
        pltpu.make_async_copy(id_ref, ids.at[r, c], s_own.at[0]),
        pltpu.make_async_copy(g_ref.at[0], raw, s_own.at[1]),
        pltpu.make_async_copy(
            a_ref.at[0, :, pl.ds(pl.multiple_of(c * rows, LANES), rows)], acts.at[r, c], s_own.at[2]),
    ]
    for cp in local:
        cp.start()
    barrier = pltpu.get_barrier_semaphore()
    for rb, cb in peers:
        pl.semaphore_signal(barrier, inc=1, device_id=(base + rx[rb], cx[cb]),
                            device_id_type=pl.DeviceIdType.MESH)
    others = []
    for h in range(1, his):
        there = lax.rem(hi + h, his)
        others.append(there * R + rx[2])
        pl.semaphore_signal(barrier, inc=1, device_id=(others[-1], c),
                            device_id_type=pl.DeviceIdType.MESH)

    local[0].wait()
    tok = ids[r, c]
    keep = jnp.transpose(jnp.broadcast_to((tok >= 0).astype(jnp.float32), (BLOCK, BLOCK)))
    keep = jnp.concatenate([keep] * (width // LANES), axis=1) > 0.5
    local[1].wait()
    for q in range(R):
        for p in range(his):
            there = lax.rem(hi + 1 + p, his)
            block = there * R + (q if p == his - 1 else q ^ 2)
            piece = raw[:, pl.ds(pl.multiple_of(block * width, LANES), width)]
            staged[q, :, p * width:(p + 1) * width] = jnp.where(
                keep, piece.astype(jnp.float32), 0.0).astype(jnp.bfloat16)
    grads[r, c] = staged[r]
    local[2].wait()

    pl.semaphore_wait(barrier, len(peers) + his - 1)

    started = []

    def send(src, dst, ssem, rsem, to):
        cp = pltpu.make_async_remote_copy(src_ref=src, dst_ref=dst, send_sem=ssem, recv_sem=rsem,
                                          device_id=to, device_id_type=pl.DeviceIdType.MESH)
        cp.start()
        started.append(cp)

    def arrive(dst, rsem):
        pltpu.make_async_copy(dst, dst, rsem).wait()

    for b in (2, 3, 1):
        send(staged.at[rx[b]], grads.at[r, c], sg_split.at[b], rg.at[r, c], (base + rx[b], c))
    for b in (1, 2, 3):
        cols = pl.ds(pl.multiple_of(cx[b] * rows, LANES), rows)
        send(a_ref.at[0, :, cols], acts.at[r, c], sa_plane.at[b], ra.at[r, c], (dp, cx[b]))
    for k, (rb, cb) in enumerate(peers):
        send(ids.at[r, c], ids.at[r, c], s_id.at[k], r_id.at[rb, cb], (base + rx[rb], cx[cb]))

    def pass_acts(cb):
        slot = acts.at[r, cx[cb]]
        send(slot, slot, sa_z.at[cb], ra.at[r, cx[cb]], (base + rx[2], c))
        send(slot, slot, sa_sib.at[cb], ra.at[r, cx[cb]], (base + rx[1], c))

    def gather_grads(rb):
        slot = grads.at[rx[rb], c]
        send(slot, slot, sg_a.at[rb], rg.at[rx[rb], c], (dp, cx[1]))
        send(slot, slot, sg_b.at[rb], rg.at[rx[rb], c], (dp, cx[2]))

    def forward_grads(rb):
        came, to = (1, 2) if rb in (0, 2) else (2, 1)
        slot = grads.at[rx[rb], cx[came]]
        arrive(slot, rg.at[rx[rb], cx[came]])
        send(slot, slot, sg_fwd.at[rb], rg.at[rx[rb], cx[came]], (dp, cx[to]))

    def forward_acts(cb):
        slot = acts.at[rx[2], cx[cb]]
        arrive(slot, ra.at[rx[2], cx[cb]])
        send(slot, slot, sa_fwd.at[cb], ra.at[rx[2], cx[cb]], (base + rx[1], c))

    gather_grads(0)
    pass_acts(0)
    for b in (1, 2, 3):
        arrive(grads.at[rx[b], c], rg.at[rx[b], c])
        gather_grads(b)
        arrive(acts.at[r, cx[b]], ra.at[r, cx[b]])
        pass_acts(b)
    seq = n * BLOCK
    wide = acts.shape[3]
    cols = grads.shape[3]
    pieces, step = outgoing.shape[1:3]
    table = shares.shape[2:]
    row_at = lax.broadcasted_iota(jnp.int32, table, 0)
    nt = (((1,), (1,)), ((), ()))

    def doc_rows(s):
        return [jnp.broadcast_to(jnp.max(ids[s, i], axis=1, keepdims=True), (1, BLOCK))
                for i in range(n)]

    def prepare(rb):
        s = rx[rb]
        for i in range(n):
            at = pl.multiple_of((s * n + i) * BLOCK, LANES)
            turned[:, pl.ds(at, BLOCK)] = jnp.transpose(acts[s, i])
        A = acts[s].reshape(seq, wide)
        gram = lax.dot_general(A, A, nt, preferred_element_type=jnp.float32)
        dr = doc_rows(s)
        along = jnp.concatenate(dr, axis=1)
        for i in range(n):
            mine = jnp.concatenate([dr[i]] * n, axis=1)
            at = slice(i * BLOCK, (i + 1) * BLOCK)
            gram_in[rb, at] = jnp.where(along == mine, gram[at], 0.0)

    def norm_step(rb, total):
        s = rx[rb]
        for cb in ((2, 3) if rb in (0, 2) else (1, 3)):
            arrive(grads.at[s, cx[cb]], rg.at[s, cx[cb]])
        G = grads[s].reshape(seq, cols)
        gram_out = lax.dot_general(G, G, nt, preferred_element_type=jnp.float32)
        v = jnp.sum(gram_in[rb] * gram_out, axis=0, keepdims=True)
        along = jnp.concatenate(doc_rows(s), axis=1)
        for b in range(docs):
            nb = jnp.sum(jnp.where(along == b, v, 0.0), axis=1, keepdims=True)
            total = jnp.where(row_at == s * docs + b, jnp.broadcast_to(nb, table), total)
        return total

    for b in range(n):
        forward_acts(b)
    for rb, cb in peers:
        arrive(ids.at[rx[rb], cx[cb]], r_id.at[rb, cb])
    for rb in (0, 2, 1, 3):
        if rb in (1, 3):
            for cb in range(n):
                arrive(acts.at[rx[rb], cx[cb]], ra.at[rx[rb], cx[cb]])
        forward_grads({0: 0, 2: 1, 1: 2, 3: 3}[rb])
        prepare(rb)
    total = jnp.zeros(table, jnp.float32)
    for rb in range(R):
        total = norm_step(rb, total)
    shares[r, c] = total
    for k, (rb, cb) in enumerate(peers):
        send(shares.at[r, c], shares.at[r, c], s_norm.at[k], r_norm.at[rb, cb],
             (base + rx[rb], cx[cb]))
    for rb, cb in peers:
        arrive(shares.at[rx[rb], cx[cb]], r_norm.at[rb, cb])
    norm = jnp.zeros(table, jnp.float32)
    for i in range(R):
        for j in range(n):
            norm = norm + shares[i, j]
    clip = clip_bound / jnp.sqrt(jnp.maximum(norm, clip_bound * clip_bound))

    lane_at = lax.broadcasted_iota(jnp.int32, (1, LANES), 1)
    own = jnp.zeros((1, LANES), jnp.float32)
    for b in range(docs):
        picked = jnp.sum(jnp.where(row_at == r * docs + b, clip, 0.0), axis=0, keepdims=True)
        own = jnp.where(lane_at == b, picked, own)
    clip_ref[...] = own[:, :docs]

    factors = []
    for s in range(R):
        dr = doc_rows(s)
        for i in range(n):
            factor = jnp.zeros((1, LANES), jnp.float32)
            for b in range(docs):
                factor = jnp.where(dr[i] == b, clip[s * docs + b:s * docs + b + 1], factor)
            factors.append(jnp.concatenate([factor] * (width // LANES), axis=1))

    def scale(p):
        at_cols = slice(p * width, (p + 1) * width)
        for k, factor in enumerate(factors):
            piece = grads[k // n, k % n, :, at_cols].astype(jnp.float32) * factor
            scaled[k * BLOCK:(k + 1) * BLOCK, at_cols] = piece.astype(jnp.bfloat16)

    for p in range(his - 1):
        scale(p)
        for k in range(pieces):
            at = slice(k * step, (k + 1) * step)
            outgoing[p, k] = jnp.dot(turned[at], scaled[:, p * width:(p + 1) * width],
                                     preferred_element_type=jnp.float32).astype(jnp.bfloat16)
            send(outgoing.at[p, k], incoming.at[p, k], s_out.at[p, k], r_out.at[p, k],
                 (others[p], c))
    scale(his - 1)
    out_ref[...] = jnp.dot(turned[...], scaled[:, (his - 1) * width:],
                           preferred_element_type=jnp.float32)
    for p in range(his - 1):
        for k in range(pieces):
            arrive(incoming.at[p, k], r_out.at[p, k])
            out_ref[k * step:(k + 1) * step] += incoming[p, k].astype(jnp.float32)
    for cp in started:
        cp.wait_send()


def group_body(activations, out_grads, segment_ids):
    n = lax.axis_size("ctx")
    size = lax.axis_size("dp")
    his = size // GROUP
    tokens, d_in = activations.shape[1:]
    d_out = out_grads.shape[2]
    rows, width = d_in // n, d_out // size
    docs = n * tokens // BLOCK // 2
    table = -(-GROUP * docs // 8) * 8
    bf, f32 = jnp.bfloat16, jnp.float32
    dma = pltpu.SemaphoreType.DMA
    vm = pl.BlockSpec(memory_space=pltpu.VMEM)
    hbm = pl.BlockSpec(memory_space=pltpu.HBM)
    pieces = rows // LANES
    peers = GROUP * n - 1
    return pl.pallas_call(
        functools.partial(kernel, docs, his, n),
        out_shape=(jax.ShapeDtypeStruct((rows, width), f32), jax.ShapeDtypeStruct((1, docs), f32)),
        in_specs=[hbm, hbm, hbm],
        out_specs=(vm, vm),
        scratch_shapes=[
            pltpu.VMEM((GROUP, n, tokens, rows), bf),
            pltpu.VMEM((GROUP, n, tokens, his * width), bf),
            pltpu.VMEM((tokens, his * GROUP * width), bf),
            pltpu.VMEM((GROUP, tokens, his * width), bf),
            pltpu.VMEM((GROUP, n, 1, tokens), jnp.int32),
            pltpu.VMEM((GROUP, n, table, LANES), f32),
            pltpu.VMEM((rows, GROUP * n * tokens), bf),
            pltpu.VMEM((GROUP, n * tokens, n * tokens), f32),
            pltpu.VMEM((GROUP * n * tokens, his * width), bf),
            pltpu.VMEM((his - 1, pieces, rows // pieces, width), bf),
            pltpu.VMEM((his - 1, pieces, rows // pieces, width), bf),
            dma((3,)),
            dma((n,)), dma((n,)), dma((n,)), dma((n,)), dma((GROUP, n)),
            dma((GROUP,)), dma((GROUP,)), dma((GROUP,)), dma((GROUP,)), dma((GROUP, n)),
            dma((peers,)), dma((GROUP, n)), dma((peers,)), dma((GROUP, n)),
            dma((his - 1, pieces)), dma((his - 1, pieces)),
        ],
        compiler_params=pltpu.CompilerParams(
            collective_id=0, has_side_effects=True, vmem_limit_bytes=53 * 1024 * 1024),
    )(activations, out_grads, segment_ids)


def body(activations, out_grads, segment_ids):
    n = lax.axis_size("ctx")
    size = lax.axis_size("dp")
    rows, width = activations.shape[2] // n, out_grads.shape[2] // size
    fits = (n == GROUP and size % GROUP == 0 and size > GROUP and activations.shape[1] == BLOCK
            and rows % LANES == 0 and width % LANES == 0)
    chosen = group_body if fits else plain_body
    return chosen(activations, out_grads, segment_ids)


def solution(mesh):
    placed = (P("dp", "ctx", None), P("dp", "ctx", None), P("dp", "ctx"))
    return jax.shard_map(
        body, mesh=mesh, in_specs=placed, out_specs=(P("ctx", "dp"), P("dp", None)), check_vma=False
    )
```
